256 devices in a mesh: leaf: 128 (over y, x, z), rhs: 2 (over core).
Axes of the slice: x: 4, y: 4, z: 8, core: 2. Of those that a mesh axis runs over, the one named last changes fastest.
Arguments:
- charges: bfloat16 [2048, 256, 256], P('leaf', None, 'rhs'), may hold values from -6 to 6
- leaf_basis: bfloat16 [2048, 256, 128], P('leaf'), may hold values from -0.375 to 0.375
- transfer3: bfloat16 [2048, 128, 128], P('leaf'), may hold values from -0.375 to 0.375
- transfer2: bfloat16 [128, 128, 128], P('leaf'), may hold values from -0.375 to 0.375
- transfer1: bfloat16 [16, 128, 128], replicated, may hold values from -0.375 to 0.375
- coupling3: bfloat16 [2048, 8, 128, 128], P('leaf'), may hold values from -0.1875 to 0.1875
- coupling2: bfloat16 [128, 4, 128, 128], P('leaf'), may hold values from -0.25 to 0.25
- coupling1: bfloat16 [16, 4, 128, 128], replicated, may hold values from -0.25 to 0.25
- coupling0: bfloat16 [4, 128, 128], replicated, may hold values from -0.5 to 0.5
- near_blocks: bfloat16 [2048, 6, 256, 256], P('leaf', 'rhs'), may hold values from -0.15625 to 0.15625
- near_list: int32 [2048, 6], P('leaf'), may hold values from 0 to 2047, as said below
- far_list3: int32 [2048, 8], P('leaf'), may hold values from 0 to 2047, as said below
- far_list2: int32 [128, 4], P('leaf'), may hold values from 0 to 127, as said below
- far_list1: int32 [16, 4], replicated, may hold values from 0 to 15, as said below
- far_list0: int32 [4], replicated, may hold values from 0 to 3, as said below
Outputs:
- potential: bfloat16 [2048, 256, 256], P('leaf', None, 'rhs')
The draws below stay inside these ranges and needn't reach their ends.
Inputs may be any that keep to these rules, and one draw needn't show every extreme that they name: `near_list`: each named leaf lies at most 8 places from the row's leaf in leaf order; the first entry is the leaf itself. `far_list3`: each named leaf lies more than 8 and at most 16 places from the row's leaf in leaf order. `far_list2`: each named node lies one or two places from the row's node. `far_list1`: never the row's node nor a node beside it in cyclic order. `far_list0`: never the row's node.
All inputs are finite; a program needn't handle non-finite values.
Results may differ from the reference program's by a relative error of at most 0.019.
Values may be sent and summed in bfloat16 or wider, within the bound.
No kernel may reach another device: no remote copies, remote signals or barrier semaphores. Data moves between devices by JAX's collectives and lax.ppermute only.
A program may use at most 128 MiB of HBM per device.

```python
import jax
import jax.numpy as jnp
from jax import lax

K = 128
BOX = 256
COLS = 256
LEAF_DEV = 16
NS = 6
F3 = 8
F2 = 4
F1 = 4
TOP1 = 16
TOP0 = 4
LEAVES = 2048
NODES2 = 128
GROUP1 = 8
N_LEAF = 128


def reflect(positions, offsets, total):
    target = positions + offsets
    return jnp.where((target < 0) | (target >= total), positions - offsets, target).astype(jnp.int32)


def draw_near_list(key, part):
    key = jax.random.fold_in(key, 11)
    half_width = LEAF_DEV // 2
    positions = jnp.arange(LEAVES, dtype=jnp.int32)[:, None]
    offsets = jax.random.randint(key, (LEAVES, NS), -half_width, half_width + 1, dtype=jnp.int32)
    offsets = offsets.at[:, 0].set(0).at[:, 1].set(-half_width).at[:, 2].set(half_width)
    return reflect(positions, offsets, LEAVES)


def draw_far_list3(key, part):
    key = jax.random.fold_in(key, 12)
    first_key, second_key = jax.random.split(key)
    half_width = LEAF_DEV // 2
    positions = jnp.arange(LEAVES, dtype=jnp.int32)[:, None]
    magnitude = jax.random.randint(first_key, (LEAVES, F3), half_width + 1, LEAF_DEV + 1, dtype=jnp.int32)
    signs = jax.random.randint(second_key, (LEAVES, F3), 0, 2, dtype=jnp.int32) * 2 - 1
    offsets = magnitude * signs
    offsets = offsets.at[:, 0].set(-LEAF_DEV).at[:, 1].set(LEAF_DEV).at[:, 2].set(half_width + 1)
    return reflect(positions, offsets, LEAVES)


def draw_far_list2(key, part):
    key = jax.random.fold_in(key, 13)
    first_key, second_key = jax.random.split(key)
    node_count = LEAVES // LEAF_DEV
    positions = jnp.arange(node_count, dtype=jnp.int32)[:, None]
    magnitude = jax.random.randint(first_key, (node_count, F2), 1, 3, dtype=jnp.int32)
    signs = jax.random.randint(second_key, (node_count, F2), 0, 2, dtype=jnp.int32) * 2 - 1
    offsets = magnitude * signs
    offsets = offsets.at[:, 0].set(-2).at[:, 1].set(1)
    return reflect(positions, offsets, node_count)


def draw_far_list1(key, part):
    key = jax.random.fold_in(key, 14)
    positions = jnp.arange(TOP1, dtype=jnp.int32)[:, None]
    jumps = jax.random.randint(key, (TOP1, F1), 0, TOP1 - 3, dtype=jnp.int32)
    jumps = jumps.at[1, 0].set(TOP1 - 4).at[2, 0].set(TOP1 - 4)
    return ((positions + 2 + jumps) % TOP1).astype(jnp.int32)


def draw_far_list0(key, part):
    key = jax.random.fold_in(key, 15)
    positions = jnp.arange(TOP0, dtype=jnp.int32)
    jumps = jax.random.randint(key, (TOP0,), 0, TOP0 - 1, dtype=jnp.int32)
    jumps = jumps.at[0].set(TOP0 - 2).at[1].set(TOP0 - 2)
    return ((positions + 1 + jumps) % TOP0).astype(jnp.int32)


def steps_of(stream_key, dims, cuts, least, high):
    gain, own = 1.0, jax.random.fold_in(stream_key, 6)
    for position, parts in cuts:
        draws = jnp.exp(jax.random.uniform(jax.random.fold_in(own, position), (parts,), jnp.float32, least / len(cuts), high / len(cuts)))
        gain = gain * jnp.repeat(draws, dims[position] // parts).reshape([-1 if axis == position else 1 for axis in range(len(dims))])
    return gain


def bell_draw(stream_key, extent, spread, limit, cuts=(), kind=jnp.bfloat16):
    values = jax.random.normal(stream_key, extent, jnp.float32) * spread
    if len(cuts) > 0:
        values = steps_of(stream_key, extent, cuts, -0.22, 0.18) * values
    return jnp.clip(values, min=-limit, max=limit).astype(kind)


def setup_inputs(seed: int = 0) -> dict:
    key_list = jax.random.split(jax.random.key(seed), 16)
    return {
        "charges": bell_draw(key_list[0], (LEAVES, BOX, COLS), 1.0, 6.0, ((0, 128), (2, 2))),
        "leaf_basis": bell_draw(key_list[1], (LEAVES, BOX, K), BOX ** -0.5, 0.375, ((0, 128),)),
        "transfer3": bell_draw(key_list[2], (LEAVES, K, K), (2 * K) ** -0.5, 0.375, ((0, 128),)),
        "transfer2": bell_draw(key_list[3], (NODES2, K, K), (2 * K) ** -0.5, 0.375, ((0, 128),)),
        "transfer1": bell_draw(key_list[4], (TOP1, K, K), (2 * K) ** -0.5, 0.375),
        "coupling3": bell_draw(key_list[5], (LEAVES, F3, K, K), (K * F3) ** -0.5, 0.1875, ((0, 128),)),
        "coupling2": bell_draw(key_list[6], (NODES2, F2, K, K), (K * F2) ** -0.5, 0.25, ((0, 128),)),
        "coupling1": bell_draw(key_list[7], (TOP1, F1, K, K), (K * F1) ** -0.5, 0.25),
        "coupling0": bell_draw(key_list[8], (TOP0, K, K), K ** -0.5, 0.5),
        "near_blocks": bell_draw(key_list[9], (LEAVES, NS, BOX, BOX), (BOX * NS) ** -0.5, 0.15625, ((0, 128), (1, 2))),
        "near_list": draw_near_list(jax.random.fold_in(key_list[15], 71), 0),
        "far_list3": draw_far_list3(jax.random.fold_in(key_list[15], 71), 0),
        "far_list2": draw_far_list2(jax.random.fold_in(key_list[15], 71), 0),
        "far_list1": draw_far_list1(jax.random.fold_in(key_list[15], 71), 0),
        "far_list0": draw_far_list0(jax.random.fold_in(key_list[15], 71), 0),
    }


def as_float(value):
    return value.astype(jnp.float32)


def reference(charges, leaf_basis, transfer3, transfer2, transfer1, coupling3, coupling2, coupling1, coupling0, near_blocks, near_list, far_list3, far_list2, far_list1, far_list0):
    def per_device(array):
        return array.reshape((N_LEAF, LEAF_DEV) + array.shape[1:])

    def leaf_moment(pieces):
        basis_part, charge_part = pieces
        return jnp.einsum('gbk,gbc->gkc', as_float(basis_part), as_float(charge_part)).astype(jnp.bfloat16)

    moments3 = lax.map(leaf_moment, (per_device(leaf_basis), per_device(charges))).reshape(LEAVES, K, COLS)

    def node_moment(pieces):
        transfer_part, moment_part = pieces
        return jnp.einsum('gkj,gkc->jc', as_float(transfer_part), as_float(moment_part)).astype(jnp.bfloat16)

    moments2 = lax.map(node_moment, (per_device(transfer3), per_device(moments3)))
    terms1 = jnp.einsum('pkj,pkc->pjc', as_float(transfer2), as_float(moments2))
    moments1 = terms1.reshape(TOP1, GROUP1, K, COLS).sum(axis=1).astype(jnp.bfloat16)
    fan_ratio = TOP1 // TOP0
    terms0 = jnp.einsum('qkj,qkc->qjc', as_float(transfer1), as_float(moments1))
    moments0 = terms0.reshape(TOP0, fan_ratio, K, COLS).sum(axis=1).astype(jnp.bfloat16)
    local0 = jnp.einsum('rkj,rjc->rkc', as_float(coupling0), as_float(jnp.take(moments0, far_list0, axis=0))).astype(jnp.bfloat16)
    parents0 = jnp.repeat(local0, fan_ratio, axis=0)
    local1 = jnp.einsum('qfkj,qfjc->qkc', as_float(coupling1), as_float(jnp.take(moments1, far_list1, axis=0)))
    local1 = (local1 + jnp.einsum('qkj,qjc->qkc', as_float(transfer1), as_float(parents0))).astype(jnp.bfloat16)
    parents1 = jnp.repeat(local1, GROUP1, axis=0)
    local2 = jnp.einsum('pfkj,pfjc->pkc', as_float(coupling2), as_float(jnp.take(moments2, far_list2, axis=0)))
    local2 = (local2 + jnp.einsum('pkj,pjc->pkc', as_float(transfer2), as_float(parents1))).astype(jnp.bfloat16)

    def leaf_local(pieces):
        coupling_part, list_part, transfer_part, parent_part = pieces
        sources = jnp.take(moments3, list_part, axis=0)
        farther = jnp.einsum('gfkj,gfjc->gkc', as_float(coupling_part), as_float(sources))
        return (farther + jnp.einsum('gkj,jc->gkc', as_float(transfer_part), as_float(parent_part))).astype(jnp.bfloat16)

    local3 = lax.map(leaf_local, (per_device(coupling3), per_device(far_list3), per_device(transfer3), local2))
    local3 = local3.reshape(LEAVES, K, COLS)

    def leaf_output(pieces):
        basis_part, local_part, block_part, list_part = pieces
        sources = jnp.take(charges, list_part, axis=0)
        result = jnp.einsum('gbk,gkc->gbc', as_float(basis_part), as_float(local_part))
        result = result + jnp.einsum('gsab,gsbc->gac', as_float(block_part), as_float(sources))
        return result.astype(jnp.bfloat16)

    potential = lax.map(leaf_output, (per_device(leaf_basis), per_device(local3), per_device(near_blocks), per_device(near_list)))
    return potential.reshape(LEAVES, BOX, COLS)
```

```python
import functools

import jax
import jax.numpy as jnp
from jax import lax
from jax.experimental import pallas as pl
from jax.experimental.pallas import tpu as pltpu
from jax.sharding import Mesh, PartitionSpec as P

TOP1 = 16
TOP0 = 4
FAN = TOP1 // TOP0
LEAF = ("y", "x", "z")
F32 = jnp.float32
BF16 = jnp.bfloat16
VMEM_LIMIT = 48 * 1024 * 1024


def dot(a, b):
    return lax.dot_general(a, b, (((1,), (0,)), ((), ())), preferred_element_type=F32)


def dot_t(a, b):
    return lax.dot_general(a, b, (((0,), (0,)), ((), ())), preferred_element_type=F32)


def shifted(block, distance):
    devices = range(lax.axis_size(LEAF))
    route = [(i - distance, i) for i in devices if i - distance in devices]
    return lax.ppermute(block, LEAF, route)


def moments_kernel(steps, per, basis, charges, transfer3, transfer2, message, spread, total):
    step = pl.program_id(0)
    share = jnp.zeros(total.shape, F32)
    for i in range(per):
        moment = dot_t(basis[i], charges[i]).astype(BF16)
        message[step * per + i] = moment
        share = share + dot_t(transfer3[i], moment)

    @pl.when(step == 0)
    def _():
        total[...] = share

    @pl.when(step > 0)
    def _():
        total[...] = total[...] + share

    @pl.when(step == steps - 1)
    def _():
        moment2 = total[...].astype(BF16)
        message[steps * per] = moment2
        term = dot_t(transfer2[0], moment2).astype(BF16)
        for i in range(spread.shape[0]):
            spread[i] = term


def moments(charges, basis, transfer3, transfer2):
    leaves, box, width = charges.shape
    rank = basis.shape[2]
    per = 4
    steps = leaves // per
    return pl.pallas_call(
        functools.partial(moments_kernel, steps, per),
        grid=(steps,),
        in_specs=[
            pl.BlockSpec((per, box, rank), lambda i: (i, 0, 0)),
            pl.BlockSpec((per, box, width), lambda i: (i, 0, 0)),
            pl.BlockSpec((per, rank, rank), lambda i: (i, 0, 0)),
            pl.BlockSpec((1, rank, rank), lambda i: (0, 0, 0)),
        ],
        out_specs=[
            pl.BlockSpec((leaves + 1, rank, width), lambda i: (0, 0, 0)),
            pl.BlockSpec((TOP1, rank, width), lambda i: (0, 0, 0)),
        ],
        out_shape=[
            jax.ShapeDtypeStruct((leaves + 1, rank, width), BF16),
            jax.ShapeDtypeStruct((TOP1, rank, width), BF16),
        ],
        scratch_shapes=[pltpu.VMEM((rank, width), F32)],
        compiler_params=pltpu.CompilerParams(vmem_limit_bytes=VMEM_LIMIT),
        cost_estimate=pl.CostEstimate(
            flops=2 * leaves * rank * width * (box + rank),
            bytes_accessed=4 * 1024 * 1024,
            transcendentals=0,
        ),
        name="moments",
    )(basis, charges, transfer3, transfer2)


def leaves_kernel(
    near_list,
    far_list,
    low,
    own,
    high,
    message_low,
    message,
    message_high,
    mine,
    theirs,
    coupling,
    near,
    far,
    sources,
    moment_sources,
    near_sems,
    far_sems,
):
    step = pl.program_id(0)
    half = low.shape[0]
    count = own.shape[0]
    first = (lax.axis_index("y") * lax.axis_size("x") + lax.axis_index("x")) * lax.axis_size(
        "z"
    ) + lax.axis_index("z")
    first = first * count
    core = lax.axis_index("core")

    near_copies = [
        pltpu.make_async_copy(low, sources.at[pl.ds(0, half)], near_sems.at[0]),
        pltpu.make_async_copy(own, sources.at[pl.ds(half, count)], near_sems.at[1]),
        pltpu.make_async_copy(high, sources.at[pl.ds(half + count, half)], near_sems.at[2]),
    ]
    far_copies = [
        pltpu.make_async_copy(
            part.at[pl.ds(0, count)], moment_sources.at[pl.ds(place * count, count)], far_sems.at[place]
        )
        for place, part in enumerate((message_low, message, message_high))
    ]

    @pl.when(step == 0)
    def _():
        for copy in near_copies + far_copies:
            copy.start()
        for copy in near_copies:
            copy.wait()

    blocks = mine.shape[1]
    left = jnp.concatenate(
        [mine[0, s] for s in range(blocks)] + [theirs[0, s] for s in range(blocks)], axis=1
    )
    places = [near_list[step, core * blocks + s] for s in range(blocks)] + [
        near_list[step, (1 - core) * blocks + s] for s in range(blocks)
    ]
    right = jnp.concatenate([sources[place - first + half] for place in places], axis=0)
    near[0] = dot(left, right)

    @pl.when(step == 0)
    def _():
        for copy in far_copies:
            copy.wait()

    partners = coupling.shape[1]
    left = jnp.concatenate([coupling[0, f] for f in range(partners)], axis=1)
    right = jnp.concatenate(
        [moment_sources[far_list[step, f] - first + count] for f in range(partners)], axis=0
    )
    far[0] = dot(left, right)


def leaf_parts(
    near_list, far_list, low, own, high, message_low, message, message_high, mine, theirs, coupling
):
    leaves, box, width = own.shape
    half = low.shape[0]
    blocks = mine.shape[1]
    partners, rank = coupling.shape[1], coupling.shape[2]
    anywhere = pl.BlockSpec(memory_space=pl.ANY)
    return pl.pallas_call(
        leaves_kernel,
        grid_spec=pltpu.PrefetchScalarGridSpec(
            num_scalar_prefetch=2,
            grid=(leaves,),
            in_specs=[anywhere] * 6
            + [
                pl.BlockSpec((1, blocks, box, box), lambda i, *_: (i, 0, 0, 0)),
                pl.BlockSpec((1, blocks, box, box), lambda i, *_: (i, 0, 0, 0)),
                pl.BlockSpec((1, partners, rank, rank), lambda i, *_: (i, 0, 0, 0)),
            ],
            out_specs=[
                pl.BlockSpec((1, box, width), lambda i, *_: (i, 0, 0)),
                pl.BlockSpec((1, rank, width), lambda i, *_: (i, 0, 0)),
            ],
            scratch_shapes=[
                pltpu.VMEM((leaves + 2 * half, box, width), BF16),
                pltpu.VMEM((3 * leaves, rank, width), BF16),
                pltpu.SemaphoreType.DMA((3,)),
                pltpu.SemaphoreType.DMA((3,)),
            ],
        ),
        out_shape=[
            jax.ShapeDtypeStruct((leaves, box, width), F32),
            jax.ShapeDtypeStruct((leaves, rank, width), F32),
        ],
        compiler_params=pltpu.CompilerParams(vmem_limit_bytes=VMEM_LIMIT),
        cost_estimate=pl.CostEstimate(
            flops=2 * leaves * width * (2 * blocks * box * box + partners * rank * rank),
            bytes_accessed=24 * 1024 * 1024,
            transcendentals=0,
        ),
        name="leaf_parts",
    )(near_list, far_list, low, own, high, message_low, message, message_high, mine, theirs, coupling)


def upper_kernel(far1, far0, terms, below, transfer1, coupling1, coupling0, spread):
    node = lax.axis_index("y") * lax.axis_size("x") + lax.axis_index("x")
    root = node // FAN
    source = far0[root]
    top = jnp.zeros(spread.shape[1:], F32)
    for i in range(FAN):
        top = top + dot_t(below[i], terms[source * FAN + i])
    local0 = dot(coupling0[0], top.astype(BF16)).astype(BF16)
    total = dot(transfer1[0], local0)
    for f in range(coupling1.shape[1]):
        total = total + dot(coupling1[0, f], terms[far1[node, f]])
    total = total.astype(BF16)
    for i in range(spread.shape[0]):
        spread[i] = total


def upper(far1, far0, terms, transfer1, coupling1, coupling0):
    count, rank, width = terms.shape
    partners = coupling1.shape[1]
    fellows = lax.axis_size("z")

    def node():
        return lax.axis_index("y") * lax.axis_size("x") + lax.axis_index("x")

    return pl.pallas_call(
        upper_kernel,
        grid_spec=pltpu.PrefetchScalarGridSpec(
            num_scalar_prefetch=2,
            grid=(1,),
            in_specs=[
                pl.BlockSpec((count, rank, width), lambda i, *_: (0, 0, 0)),
                pl.BlockSpec((FAN, rank, rank), lambda i, far1, far0: (far0[node() // FAN], 0, 0)),
                pl.BlockSpec((1, rank, rank), lambda i, *_: (node(), 0, 0)),
                pl.BlockSpec((1, partners, rank, rank), lambda i, *_: (node(), 0, 0, 0)),
                pl.BlockSpec((1, rank, rank), lambda i, *_: (node() // FAN, 0, 0)),
            ],
            out_specs=pl.BlockSpec((fellows, rank, width), lambda i, *_: (0, 0, 0)),
        ),
        out_shape=jax.ShapeDtypeStruct((fellows, rank, width), BF16),
        compiler_params=pltpu.CompilerParams(vmem_limit_bytes=VMEM_LIMIT),
        cost_estimate=pl.CostEstimate(
            flops=2 * 10 * rank * rank * width, bytes_accessed=1024 * 1024, transcendentals=0
        ),
        name="upper",
    )(far1, far0, terms, transfer1, transfer1, coupling1, coupling0)


def finish_kernel(
    per,
    far2,
    pieces,
    down1,
    up1,
    down2,
    up2,
    transfer2,
    coupling2,
    basis,
    transfer3,
    near,
    far,
    potential,
    local2,
):
    step = pl.program_id(0)

    @pl.when(step == 0)
    def _():
        total = pieces[0].astype(F32)
        for i in range(1, pieces.shape[0]):
            total = total + pieces[i].astype(F32)
        result = dot(transfer2[0], total.astype(BF16))
        device = (lax.axis_index("y") * lax.axis_size("x") + lax.axis_index("x")) * lax.axis_size(
            "z"
        ) + lax.axis_index("z")
        for f in range(coupling2.shape[1]):
            offset = far2[0, f] - device
            source = jnp.where(
                offset < 0,
                jnp.where(offset == -1, down1[0], down2[...]),
                jnp.where(offset == 1, up1[0], up2[...]),
            )
            result = result + dot(coupling2[0, f], source)
        local2[...] = result.astype(BF16)

    parent = local2[...]
    for i in range(per):
        local3 = (far[i] + dot(transfer3[i], parent)).astype(BF16)
        potential[i] = (near[i] + dot(basis[i], local3)).astype(BF16)


def finish(far2, pieces, down1, up1, down2, up2, transfer2, coupling2, basis, transfer3, near, far):
    leaves, box, width = near.shape
    rank = far.shape[1]
    partners = coupling2.shape[1]
    per = 4
    fixed = lambda i, *_: (0, 0, 0)
    along = lambda i, *_: (i, 0, 0)
    last = lambda i, *_: (leaves, 0, 0)
    return pl.pallas_call(
        functools.partial(finish_kernel, per),
        grid_spec=pltpu.PrefetchScalarGridSpec(
            num_scalar_prefetch=1,
            grid=(leaves // per,),
            in_specs=[
                pl.BlockSpec(pieces.shape, fixed),
                pl.BlockSpec((1, rank, width), last),
                pl.BlockSpec((1, rank, width), last),
                pl.BlockSpec((rank, width), lambda i, *_: (0, 0)),
                pl.BlockSpec((rank, width), lambda i, *_: (0, 0)),
                pl.BlockSpec((1, rank, rank), fixed),
                pl.BlockSpec((1, partners, rank, rank), lambda i, *_: (0, 0, 0, 0)),
                pl.BlockSpec((per, box, rank), along),
                pl.BlockSpec((per, rank, rank), along),
                pl.BlockSpec((per, box, width), along),
                pl.BlockSpec((per, rank, width), along),
            ],
            out_specs=pl.BlockSpec((per, box, width), along),
            scratch_shapes=[pltpu.VMEM((rank, width), BF16)],
        ),
        out_shape=jax.ShapeDtypeStruct((leaves, box, width), BF16),
        compiler_params=pltpu.CompilerParams(vmem_limit_bytes=VMEM_LIMIT),
        cost_estimate=pl.CostEstimate(
            flops=2 * leaves * rank * width * (box + rank),
            bytes_accessed=6 * 1024 * 1024,
            transcendentals=0,
        ),
        name="finish",
    )(far2, pieces, down1, up1, down2, up2, transfer2, coupling2, basis, transfer3, near, far)


def body(
    charges,
    leaf_basis,
    transfer3,
    transfer2,
    transfer1,
    coupling3,
    coupling2,
    coupling1,
    coupling0,
    near_blocks,
    near_list,
    far_list3,
    far_list2,
    far_list1,
    far_list0,
):
    leaves = charges.shape[0]
    half = leaves // 2
    other_blocks = lax.ppermute(near_blocks, "core", [(0, 1), (1, 0)])
    low = shifted(charges[leaves - half :], 1)
    high = shifted(charges[:half], -1)
    message, spread = moments(charges, leaf_basis, transfer3, transfer2)
    terms = lax.all_to_all(spread, ("y", "x"), 0, 0, tiled=True)
    message_low = shifted(message, 1)
    message_high = shifted(message, -1)
    down2 = shifted(message[leaves], 2)
    up2 = shifted(message[leaves], -2)
    near, far = leaf_parts(
        near_list,
        far_list3,
        low,
        charges,
        high,
        message_low,
        message,
        message_high,
        near_blocks,
        other_blocks,
        coupling3,
    )
    pieces = upper(far_list1, far_list0, terms, transfer1, coupling1, coupling0)
    pieces = lax.all_to_all(pieces, "z", 0, 0, tiled=True)
    return finish(
        far_list2,
        pieces,
        message_low,
        message_high,
        down2,
        up2,
        transfer2,
        coupling2,
        leaf_basis,
        transfer3,
        near,
        far,
    )


def solution(mesh):
    grid = Mesh(mesh.devices.reshape(4, 4, 8, 2), ("y", "x", "z", "core"))
    placed = (
        P(LEAF, None, "core"),
        P(LEAF, None, None),
        P(LEAF, None, None),
        P(LEAF, None, None),
        P(),
        P(LEAF, None, None, None),
        P(LEAF, None, None, None),
        P(),
        P(),
        P(LEAF, "core", None, None),
        P(LEAF, None),
        P(LEAF, None),
        P(LEAF, None),
        P(),
        P(),
    )
    return jax.shard_map(
        body, mesh=grid, in_specs=placed, out_specs=P(LEAF, None, "core"), check_vma=False
    )
```

```python
import functools

import jax
import jax.numpy as jnp
from jax import lax
from jax.experimental import pallas as pl
from jax.experimental.pallas import tpu as pltpu
from jax.sharding import Mesh, PartitionSpec as P

TOP1 = 16
TOP0 = 4
FAN = TOP1 // TOP0
LEAF = ("y", "x", "z")
EVERY = ("y", "x", "z", "core")
F32 = jnp.float32
BF16 = jnp.bfloat16
MIB = 1024 * 1024
HBM = pl.BlockSpec(memory_space=pltpu.HBM)
ANY = pl.BlockSpec(memory_space=pl.ANY)
VMEM = pl.BlockSpec(memory_space=pltpu.VMEM)
SMEM = pl.BlockSpec(memory_space=pltpu.SMEM)


def dot(a, b):
    return lax.dot_general(a, b, (((1,), (0,)), ((), ())), preferred_element_type=F32)


def dot_t(a, b):
    return lax.dot_general(a, b, (((0,), (0,)), ((), ())), preferred_element_type=F32)


def rows(start, size):
    return pl.ds(pl.multiple_of(start, 128), size)


def node_index():
    return lax.axis_index("y") * lax.axis_size("x") + lax.axis_index("x")


def device_index():
    return node_index() * lax.axis_size("z") + lax.axis_index("z")


def swapped(block):
    return lax.ppermute(block, "core", [(0, 1), (1, 0)])


def in_hbm(*arrays):
    return [pltpu.with_memory_space_constraint(array, pltpu.HBM) for array in arrays]


def exchanged(block, odd):
    count = lax.axis_size(LEAF)
    pairs = [(i, i + 1) for i in range(1 if odd else 0, count - 1, 2)]
    return lax.ppermute(block, LEAF, pairs + [(b, a) for a, b in pairs])


def settings(limit, flops, moved):
    return dict(
        compiler_params=pltpu.CompilerParams(vmem_limit_bytes=limit * MIB),
        cost_estimate=pl.CostEstimate(flops=flops, bytes_accessed=moved, transcendentals=0),
    )


def edges_kernel(charges, first, second, sems):
    half = first.shape[0]
    odd = lax.rem(device_index(), 2)
    copies = [
        pltpu.make_async_copy(charges.at[rows((1 - odd) * half, half)], first, sems.at[0]),
        pltpu.make_async_copy(charges.at[rows(odd * half, half)], second, sems.at[1]),
    ]
    for copy in copies:
        copy.start()
    for copy in copies:
        copy.wait()


def edges(charges):
    half = charges.shape[0] // 2
    shape = jax.ShapeDtypeStruct((half, charges.shape[1]), BF16)
    return pl.pallas_call(
        edges_kernel,
        in_specs=[HBM],
        out_specs=[ANY, ANY],
        out_shape=[shape, shape],
        scratch_shapes=[pltpu.SemaphoreType.DMA((2,))],
        name="edges",
        **settings(8, 0, 2 * MIB),
    )(*in_hbm(charges))


def moments_kernel(
    groups,
    charges,
    basis,
    transfer3,
    transfer2,
    after,
    moment_out,
    moment2_out,
    spread,
    charge_buf,
    basis_buf,
    transfer3_buf,
    transfer2_buf,
    moment_buf,
    in_sems,
    out_sems,
):
    leaves, box, rank = basis.shape
    per = leaves // groups
    loads = []
    for i in range(groups):
        span = pl.ds(i * per * box, per * box)
        part = pl.ds(i * per, per)
        loads.append(
            [
                pltpu.make_async_copy(charges.at[span], charge_buf.at[span], in_sems.at[0, i]),
                pltpu.make_async_copy(basis.at[part], basis_buf.at[part], in_sems.at[1, i]),
                pltpu.make_async_copy(transfer3.at[part], transfer3_buf.at[part], in_sems.at[2, i]),
            ]
        )
    last = pltpu.make_async_copy(transfer2, transfer2_buf, in_sems.at[0, groups])
    for load in loads:
        for copy in load:
            copy.start()
    last.start()
    total = None
    stores = []
    for i in range(groups):
        for copy in loads[i]:
            copy.wait()
        for leaf in range(i * per, (i + 1) * per):
            moment = dot_t(basis_buf[leaf], charge_buf[pl.ds(leaf * box, box)]).astype(BF16)
            moment_buf[pl.ds(leaf * rank, rank)] = moment
            share = dot_t(transfer3_buf[leaf], moment)
            total = share if total is None else total + share
        size = per * rank
        if i == groups - 1:
            moment2 = total.astype(BF16)
            moment_buf[pl.ds(leaves * rank, rank)] = moment2
            moment2_out[...] = moment2
            size = size + rank
        span = pl.ds(i * per * rank, size)
        copy = pltpu.make_async_copy(moment_buf.at[span], moment_out.at[span], out_sems.at[i])
        copy.start()
        stores.append(copy)
    last.wait()
    term = dot_t(transfer2_buf[0], moment2).astype(BF16)
    for i in range(spread.shape[0]):
        spread[i] = term
    for copy in stores:
        copy.wait()


def moments(charges, basis, transfer3, transfer2, after):
    leaves, box, rank = basis.shape
    width = charges.shape[1]
    groups = 4
    return pl.pallas_call(
        functools.partial(moments_kernel, groups),
        in_specs=[HBM] * 5,
        out_specs=[ANY, VMEM, VMEM],
        out_shape=[
            jax.ShapeDtypeStruct(((leaves + 1) * rank, width), BF16),
            jax.ShapeDtypeStruct((rank, width), BF16),
            jax.ShapeDtypeStruct((TOP1, rank, width), BF16),
        ],
        scratch_shapes=[
            pltpu.VMEM((leaves * box, width), BF16),
            pltpu.VMEM((leaves, box, rank), BF16),
            pltpu.VMEM((leaves, rank, rank), BF16),
            pltpu.VMEM((1, rank, rank), BF16),
            pltpu.VMEM(((leaves + 1) * rank, width), BF16),
            pltpu.SemaphoreType.DMA((3, groups + 1)),
            pltpu.SemaphoreType.DMA((groups,)),
        ],
        name="moments",
        **settings(12, 2 * leaves * rank * width * (box + rank), 6 * MIB),
    )(*in_hbm(charges, basis, transfer3, transfer2, after))


def weights_kernel(
    far0,
    basis,
    transfer3,
    transfer1,
    coupling1,
    coupling0,
    joined,
    upper,
    basis_buf,
    transfer3_buf,
    below_buf,
    own_buf,
    coupling1_buf,
    coupling0_buf,
    sems,
):
    leaves, box, rank = basis.shape
    partners = coupling1.shape[1]
    node = node_index()
    root = node // FAN
    copies = [
        pltpu.make_async_copy(transfer1.at[pl.ds(far0[root] * FAN, FAN)], below_buf, sems.at[0]),
        pltpu.make_async_copy(transfer1.at[pl.ds(node, 1)], own_buf, sems.at[1]),
        pltpu.make_async_copy(coupling1.at[pl.ds(node, 1)], coupling1_buf, sems.at[2]),
        pltpu.make_async_copy(coupling0.at[pl.ds(root, 1)], coupling0_buf, sems.at[3]),
        pltpu.make_async_copy(basis, basis_buf, sems.at[4]),
        pltpu.make_async_copy(transfer3, transfer3_buf, sems.at[5]),
    ]
    for copy in copies:
        copy.start()
    for copy in copies[:4]:
        copy.wait()
    through = dot(own_buf[0], coupling0_buf[0]).astype(BF16)
    for i in range(FAN):
        upper[:, i * rank : (i + 1) * rank] = lax.dot_general(
            through, below_buf[i], (((1,), (1,)), ((), ())), preferred_element_type=F32
        ).astype(BF16)
    for f in range(partners):
        upper[:, (FAN + f) * rank : (FAN + f + 1) * rank] = coupling1_buf[0, f]
    for copy in copies[4:]:
        copy.wait()
    for leaf in range(leaves):
        joined[leaf * box : (leaf + 1) * box] = dot(basis_buf[leaf], transfer3_buf[leaf]).astype(BF16)


def weights(far0, basis, transfer3, transfer1, coupling1, coupling0):
    leaves, box, rank = basis.shape
    partners = coupling1.shape[1]
    return pl.pallas_call(
        weights_kernel,
        in_specs=[SMEM] + [HBM] * 5,
        out_specs=[VMEM, VMEM],
        out_shape=[
            jax.ShapeDtypeStruct((leaves * box, rank), BF16),
            jax.ShapeDtypeStruct((rank, (FAN + partners) * rank), BF16),
        ],
        scratch_shapes=[
            pltpu.VMEM((leaves, box, rank), BF16),
            pltpu.VMEM((leaves, rank, rank), BF16),
            pltpu.VMEM((FAN, rank, rank), BF16),
            pltpu.VMEM((1, rank, rank), BF16),
            pltpu.VMEM((1, partners, rank, rank), BF16),
            pltpu.VMEM((1, rank, rank), BF16),
            pltpu.SemaphoreType.DMA((6,)),
        ],
        name="weights",
        **settings(8, 2 * leaves * box * rank * rank, 3 * MIB),
    )(far0, *in_hbm(basis, transfer3, transfer1, coupling1, coupling0))


def upper_kernel(far1, far0, terms, left, spread):
    node = node_index()
    partners = far1.shape[1]
    source = far0[node // FAN]
    right = jnp.concatenate(
        [terms[source * FAN + i] for i in range(FAN)] + [terms[far1[node, f]] for f in range(partners)],
        axis=0,
    )
    total = dot(left[...], right).astype(BF16)
    for i in range(spread.shape[0]):
        spread[i] = total


def upper(far1, far0, terms, left):
    rank, width = terms.shape[1:]
    fellows = lax.axis_size("z")
    return pl.pallas_call(
        upper_kernel,
        in_specs=[SMEM, SMEM, VMEM, VMEM],
        out_specs=VMEM,
        out_shape=jax.ShapeDtypeStruct((fellows, rank, width), BF16),
        name="upper",
        **settings(8, 2 * left.shape[1] * rank * width, MIB),
    )(far1, far0, terms, left)


def near_kernel(
    near_list,
    first_edge,
    own,
    second_edge,
    mine,
    theirs,
    partial,
    charge_buf,
    mine_buf,
    theirs_buf,
    source_sems,
    sems,
):
    leaves, blocks, box, _ = mine.shape
    edge = first_edge.shape[0]
    device = device_index()
    odd = lax.rem(device, 2)
    first = device * leaves
    core = lax.axis_index("core")
    far_end = edge + leaves * box
    sources = [
        (first_edge, charge_buf.at[rows((1 - odd) * far_end, edge)]),
        (own, charge_buf.at[pl.ds(edge, leaves * box)]),
        (second_edge, charge_buf.at[rows(odd * far_end, edge)]),
    ]
    sources = [
        pltpu.make_async_copy(a, b, source_sems.at[i]) for i, (a, b) in enumerate(sources)
    ]

    def loads(leaf):
        return [
            pltpu.make_async_copy(mine.at[leaf], mine_buf.at[leaf], sems.at[0, leaf]),
            pltpu.make_async_copy(theirs.at[leaf], theirs_buf.at[leaf], sems.at[1, leaf]),
        ]

    def begin(leaf, carry):
        for copy in loads(leaf):
            copy.start()
        return carry

    for copy in sources:
        copy.start()
    lax.fori_loop(0, leaves, begin, 0)
    for copy in sources:
        copy.wait()

    def work(leaf, carry):
        for copy in loads(leaf):
            copy.wait()
        places = [near_list[leaf, core * blocks + s] for s in range(blocks)] + [
            near_list[leaf, (1 - core) * blocks + s] for s in range(blocks)
        ]
        left = jnp.concatenate(
            [mine_buf[leaf, s] for s in range(blocks)] + [theirs_buf[leaf, s] for s in range(blocks)],
            axis=1,
        )
        right = jnp.concatenate(
            [charge_buf[rows((place - first) * box + edge, box)] for place in places], axis=0
        )
        partial[rows(leaf * box, box)] = dot(left, right).astype(BF16)
        return carry

    lax.fori_loop(0, leaves, work, 0)


def near_parts(near_list, first_edge, own, second_edge, mine, theirs):
    leaves, blocks, box, _ = mine.shape
    width = own.shape[1]
    return pl.pallas_call(
        near_kernel,
        in_specs=[SMEM] + [HBM] * 5,
        out_specs=VMEM,
        out_shape=jax.ShapeDtypeStruct((leaves * box, width), BF16),
        scratch_shapes=[
            pltpu.VMEM((2 * leaves * box, width), BF16),
            pltpu.VMEM(mine.shape, BF16),
            pltpu.VMEM(mine.shape, BF16),
            pltpu.SemaphoreType.DMA((3,)),
            pltpu.SemaphoreType.DMA((2, leaves)),
        ],
        name="near_parts",
        **settings(24, 2 * leaves * width * 2 * blocks * box * box, 16 * MIB),
    )(near_list, *in_hbm(first_edge, own, second_edge, mine, theirs))


def far_kernel(
    far_list,
    far2,
    first_message,
    message,
    second_message,
    beside,
    across,
    coupling,
    basis,
    coupling2,
    partial,
    result,
    result2,
    moment_buf,
    moment2_buf,
    coupling_buf,
    basis_buf,
    coupling2_buf,
    source_sems,
    sems,
    other_sems,
):
    leaves, partners, rank, _ = coupling.shape
    box = basis.shape[1]
    tall = leaves * rank
    device = device_index()
    odd = lax.rem(device, 2)
    first = device * leaves
    core = lax.axis_index("core")
    sources = [
        (first_message.at[pl.ds(0, tall)], moment_buf.at[rows((1 - odd) * (2 * tall), tall)]),
        (message.at[pl.ds(0, tall)], moment_buf.at[pl.ds(tall, tall)]),
        (second_message.at[pl.ds(0, tall)], moment_buf.at[rows(odd * (2 * tall), tall)]),
    ]
    sources = [
        pltpu.make_async_copy(a, b, source_sems.at[i]) for i, (a, b) in enumerate(sources)
    ]
    others = [
        (basis, basis_buf),
        (coupling2, coupling2_buf),
        (
            first_message.at[pl.ds(tall, rank)],
            moment2_buf.at[rows((1 + 2 * (1 - odd)) * rank, rank)],
        ),
        (second_message.at[pl.ds(tall, rank)], moment2_buf.at[rows((1 + 2 * odd) * rank, rank)]),
        (beside.at[pl.ds(0, rank)], moment2_buf.at[rows(core * (4 * rank), rank)]),
        (across, moment2_buf.at[rows((1 - core) * (4 * rank), rank)]),
    ]
    others = [pltpu.make_async_copy(a, b, other_sems.at[i]) for i, (a, b) in enumerate(others)]

    def load(leaf):
        return pltpu.make_async_copy(coupling.at[leaf], coupling_buf.at[leaf], sems.at[leaf])

    def begin(leaf, carry):
        load(leaf).start()
        return carry

    for copy in sources:
        copy.start()
    lax.fori_loop(0, leaves, begin, 0)
    for copy in others:
        copy.start()
    for copy in sources:
        copy.wait()
    others[0].wait()

    def work(leaf, carry):
        load(leaf).wait()
        left = jnp.concatenate([coupling_buf[leaf, f] for f in range(partners)], axis=1)
        right = jnp.concatenate(
            [
                moment_buf[rows((far_list[leaf, f] - first + leaves) * rank, rank)]
                for f in range(partners)
            ],
            axis=0,
        )
        far = dot(left, right).astype(BF16)
        span = rows(leaf * box, box)
        result[span] = (partial[span].astype(F32) + dot(basis_buf[leaf], far)).astype(BF16)
        return carry

    lax.fori_loop(0, leaves, work, 0)
    for copy in others[1:]:
        copy.wait()
    total = None
    for f in range(far2.shape[1]):
        share = dot(
            coupling2_buf[0, f], moment2_buf[rows((far2[0, f] - device + 2) * rank, rank)]
        )
        total = share if total is None else total + share
    result2[...] = total


def far_parts(
    far_list, far2, first_message, message, second_message, beside, across, coupling, basis, coupling2, partial
):
    leaves, partners, rank, _ = coupling.shape
    box, width = basis.shape[1], partial.shape[1]
    return pl.pallas_call(
        far_kernel,
        in_specs=[SMEM] * 2 + [HBM] * 3 + [ANY] * 2 + [HBM] * 3 + [VMEM],
        out_specs=[VMEM, VMEM],
        out_shape=[
            jax.ShapeDtypeStruct((leaves * box, width), BF16),
            jax.ShapeDtypeStruct((rank, width), F32),
        ],
        scratch_shapes=[
            pltpu.VMEM((3 * leaves * rank, width), BF16),
            pltpu.VMEM((5 * rank, width), BF16),
            pltpu.VMEM(coupling.shape, BF16),
            pltpu.VMEM(basis.shape, BF16),
            pltpu.VMEM(coupling2.shape, BF16),
            pltpu.SemaphoreType.DMA((3,)),
            pltpu.SemaphoreType.DMA((leaves,)),
            pltpu.SemaphoreType.DMA((6,)),
        ],
        name="far_parts",
        **settings(16, 2 * leaves * width * (partners * rank * rank + box * rank), 8 * MIB),
    )(
        far_list,
        far2,
        *in_hbm(first_message, message, second_message),
        beside,
        across,
        *in_hbm(coupling, basis, coupling2),
        partial,
    )


def finish_kernel(
    groups,
    pieces,
    partial2,
    transfer2,
    partial,
    joined,
    potential,
    transfer2_buf,
    partial_buf,
    joined_buf,
    result_buf,
    sems,
    out_sems,
):
    size = partial.shape[0] // groups
    first = pltpu.make_async_copy(transfer2, transfer2_buf, sems.at[0, groups])
    first.start()
    loads = []
    for i in range(groups):
        span = pl.ds(i * size, size)
        loads.append(
            [
                pltpu.make_async_copy(partial.at[span], partial_buf.at[span], sems.at[0, i]),
                pltpu.make_async_copy(joined.at[span], joined_buf.at[span], sems.at[1, i]),
            ]
        )
    for load in loads:
        for copy in load:
            copy.start()
    total = pieces[0].astype(F32)
    for i in range(1, pieces.shape[0]):
        total = total + pieces[i].astype(F32)
    first.wait()
    local2 = (partial2[...] + dot(transfer2_buf[0], total.astype(BF16))).astype(BF16)
    stores = []
    for i in range(groups):
        for copy in loads[i]:
            copy.wait()
        span = pl.ds(i * size, size)
        result_buf[span] = (partial_buf[span].astype(F32) + dot(joined_buf[span], local2)).astype(BF16)
        copy = pltpu.make_async_copy(result_buf.at[span], potential.at[span], out_sems.at[i])
        copy.start()
        stores.append(copy)
    for copy in stores:
        copy.wait()


def finish(pieces, partial2, transfer2, partial, joined):
    groups = 4
    return pl.pallas_call(
        functools.partial(finish_kernel, groups),
        in_specs=[VMEM, VMEM, HBM, ANY, ANY],
        out_specs=HBM,
        out_shape=jax.ShapeDtypeStruct(partial.shape, BF16),
        scratch_shapes=[
            pltpu.VMEM(transfer2.shape, BF16),
            pltpu.VMEM(partial.shape, BF16),
            pltpu.VMEM(joined.shape, BF16),
            pltpu.VMEM(partial.shape, BF16),
            pltpu.SemaphoreType.DMA((2, groups + 1)),
            pltpu.SemaphoreType.DMA((groups,)),
        ],
        name="finish",
        **settings(12, 2 * partial.shape[0] * partial.shape[1] * joined.shape[1], 4 * MIB),
    )(pieces, partial2, *in_hbm(transfer2), partial, joined)


def two_away(moment2):
    count = lax.axis_size(LEAF)
    both = jnp.concatenate([moment2, swapped(moment2)], axis=0)
    route = [(2 * i, 2 * (i + 2)) for i in range(count - 2)]
    route += [(2 * i + 1, 2 * (i - 2) + 1) for i in range(2, count)]
    beside = lax.ppermute(both, EVERY, route)
    return beside, swapped(beside[moment2.shape[0] :])


def body(
    charges,
    leaf_basis,
    transfer3,
    transfer2,
    transfer1,
    coupling3,
    coupling2,
    coupling1,
    coupling0,
    near_blocks,
    near_list,
    far_list3,
    far_list2,
    far_list1,
    far_list0,
):
    leaves, box, width = charges.shape
    other_blocks = swapped(near_blocks)
    flat = charges.reshape(leaves * box, width)
    edge_one, edge_two = edges(flat)
    first_edge = exchanged(edge_one, False)
    second_edge = exchanged(edge_two, True)
    message, moment2, spread = moments(flat, leaf_basis, transfer3, transfer2, edge_one)
    terms = lax.all_to_all(spread, ("y", "x"), 0, 0, tiled=True)
    first_message = exchanged(message, False)
    second_message = exchanged(message, True)
    beside, across = two_away(moment2)
    joined, left = weights(far_list0, leaf_basis, transfer3, transfer1, coupling1, coupling0)
    pieces = upper(far_list1, far_list0, terms, left)
    pieces = lax.all_to_all(pieces, "z", 0, 0, tiled=True)
    partial = near_parts(near_list, first_edge, flat, second_edge, near_blocks, other_blocks)
    partial, partial2 = far_parts(
        far_list3,
        far_list2,
        first_message,
        message,
        second_message,
        beside,
        across,
        coupling3,
        leaf_basis,
        coupling2,
        partial,
    )
    potential = finish(pieces, partial2, transfer2, partial, joined)
    return potential.reshape(leaves, box, width)


def solution(mesh):
    grid = Mesh(mesh.devices.reshape(4, 4, 8, 2), ("y", "x", "z", "core"))
    placed = (
        P(LEAF, None, "core"),
        P(LEAF, None, None),
        P(LEAF, None, None),
        P(LEAF, None, None),
        P(),
        P(LEAF, None, None, None),
        P(LEAF, None, None, None),
        P(),
        P(),
        P(LEAF, "core", None, None),
        P(LEAF, None),
        P(LEAF, None),
        P(LEAF, None),
        P(),
        P(),
    )
    return jax.shard_map(
        body, mesh=grid, in_specs=placed, out_specs=P(LEAF, None, "core"), check_vma=False
    )
```

```python
import functools

import jax
import jax.numpy as jnp
from jax import lax
from jax.experimental import pallas as pl
from jax.experimental.pallas import tpu as pltpu
from jax.sharding import Mesh, PartitionSpec as P

TOP1 = 16
TOP0 = 4
FAN = TOP1 // TOP0
LEAF = ("y", "x", "z")
F32 = jnp.float32
BF16 = jnp.bfloat16
MIB = 1024 * 1024
NEAR_WORK = 1
FAR_WORK = 20
UPPER_WORK = 1
MOMENTS_WORK = 1
HBM = pl.BlockSpec(memory_space=pltpu.HBM)
ANY = pl.BlockSpec(memory_space=pl.ANY)
VMEM = pl.BlockSpec(memory_space=pltpu.VMEM)
SMEM = pl.BlockSpec(memory_space=pltpu.SMEM)


def dot(a, b):
    return lax.dot_general(a, b, (((1,), (0,)), ((), ())), preferred_element_type=F32)


def dot_t(a, b):
    return lax.dot_general(a, b, (((0,), (0,)), ((), ())), preferred_element_type=F32)


def rows(start, size):
    return pl.ds(pl.multiple_of(start, 128), size)


def node_index():
    return lax.axis_index("y") * lax.axis_size("x") + lax.axis_index("x")


def device_index():
    return node_index() * lax.axis_size("z") + lax.axis_index("z")


def swapped(block):
    return lax.ppermute(block, "core", [(0, 1), (1, 0)])


def in_hbm(*arrays):
    return [pltpu.with_memory_space_constraint(array, pltpu.HBM) for array in arrays]


def exchanged(block, odd):
    count = lax.axis_size(LEAF)
    pairs = [(i, i + 1) for i in range(1 if odd else 0, count - 1, 2)]
    return lax.ppermute(block, LEAF, pairs + [(b, a) for a, b in pairs])


def settings(limit, work=1):
    return dict(
        compiler_params=pltpu.CompilerParams(vmem_limit_bytes=limit * MIB),
        cost_estimate=pl.CostEstimate(flops=work * 10**9, bytes_accessed=1000, transcendentals=0),
    )


def streamed(count, depth, copies, work):
    def begin(i):
        for copy in copies(i):
            copy.start()

    def step(i, carry):
        for copy in copies(i):
            copy.wait()
        pl.when(i + depth < count)(lambda: begin(i + depth))
        work(i)
        return carry

    def first(i, carry):
        begin(i)
        return carry

    lax.fori_loop(0, min(depth, count), first, 0)
    return lambda: lax.fori_loop(0, count, step, 0)


def edges_kernel(charges, first, second, sems):
    half = first.shape[0]
    odd = lax.rem(device_index(), 2)
    copies = [
        pltpu.make_async_copy(charges.at[rows((1 - odd) * half, half)], first, sems.at[0]),
        pltpu.make_async_copy(charges.at[rows(odd * half, half)], second, sems.at[1]),
    ]
    for copy in copies:
        copy.start()
    for copy in copies:
        copy.wait()


def edges(charges):
    half = charges.shape[0] // 2
    shape = jax.ShapeDtypeStruct((half, charges.shape[1]), BF16)
    return pl.pallas_call(
        edges_kernel,
        in_specs=[HBM],
        out_specs=[ANY, ANY],
        out_shape=[shape, shape],
        scratch_shapes=[pltpu.SemaphoreType.DMA((2,))],
        name="edges",
        **settings(8),
    )(*in_hbm(charges))


def moments_kernel(
    groups,
    charges,
    basis,
    transfer3,
    transfer2,
    transfer1,
    coupling1,
    coupling0,
    after,
    moment_out,
    moment2_out,
    spread,
    below,
    own_coupling1,
    own_coupling0,
    charge_buf,
    basis_buf,
    transfer3_buf,
    transfer2_buf,
    moment_buf,
    in_sems,
    out_sems,
    upper_sems,
):
    leaves, box, rank = basis.shape
    per = leaves // groups
    node = node_index()
    root = node // FAN
    loads = []
    for i in range(groups):
        span = pl.ds(i * per * box, per * box)
        part = pl.ds(i * per, per)
        loads.append(
            [
                pltpu.make_async_copy(charges.at[span], charge_buf.at[span], in_sems.at[0, i]),
                pltpu.make_async_copy(basis.at[part], basis_buf.at[part], in_sems.at[1, i]),
            ]
        )
    extra = [
        (transfer3, transfer3_buf),
        (transfer2, transfer2_buf),
        (transfer1, below),
        (coupling1.at[pl.ds(node, 1)], own_coupling1),
        (coupling0.at[pl.ds(root, 1)], own_coupling0),
    ]
    extra = [pltpu.make_async_copy(a, b, upper_sems.at[i]) for i, (a, b) in enumerate(extra)]
    for load in loads:
        for copy in load:
            copy.start()
    for copy in extra:
        copy.start()
    stores = []
    for i in range(groups):
        for copy in loads[i]:
            copy.wait()
        for leaf in range(i * per, (i + 1) * per):
            moment = dot_t(basis_buf[leaf], charge_buf[pl.ds(leaf * box, box)])
            moment_buf[pl.ds(leaf * rank, rank)] = moment.astype(BF16)
        span = pl.ds(i * per * rank, per * rank)
        copy = pltpu.make_async_copy(moment_buf.at[span], moment_out.at[span], out_sems.at[i])
        copy.start()
        stores.append(copy)
    for copy in extra[:2]:
        copy.wait()
    moment2 = dot_t(transfer3_buf[...], moment_buf[pl.ds(0, leaves * rank)]).astype(BF16)
    moment_buf[pl.ds(leaves * rank, rank)] = moment2
    span = pl.ds(leaves * rank, rank)
    copy = pltpu.make_async_copy(moment_buf.at[span], moment_out.at[span], out_sems.at[groups])
    copy.start()
    stores.append(copy)
    moment2_out[...] = moment2
    term = dot_t(transfer2_buf[0], moment2).astype(BF16)
    for i in range(spread.shape[0]):
        spread[i] = term
    for copy in stores + extra[2:]:
        copy.wait()


def moments(charges, basis, transfer3, transfer2, transfer1, coupling1, coupling0, after):
    leaves, box, rank = basis.shape
    width = charges.shape[1]
    partners = coupling1.shape[1]
    groups = 4
    return pl.pallas_call(
        functools.partial(moments_kernel, groups),
        in_specs=[HBM] * 7 + [ANY],
        out_specs=[ANY] + [VMEM] * 5,
        out_shape=[
            jax.ShapeDtypeStruct(((leaves + 1) * rank, width), BF16),
            jax.ShapeDtypeStruct((rank, width), BF16),
            jax.ShapeDtypeStruct((TOP1, rank, width), BF16),
            jax.ShapeDtypeStruct(transfer1.shape, BF16),
            jax.ShapeDtypeStruct((1, partners, rank, rank), BF16),
            jax.ShapeDtypeStruct((1, rank, rank), BF16),
        ],
        scratch_shapes=[
            pltpu.VMEM((leaves * box, width), BF16),
            pltpu.VMEM((leaves, box, rank), BF16),
            pltpu.VMEM((leaves * rank, rank), BF16),
            pltpu.VMEM((1, rank, rank), BF16),
            pltpu.VMEM(((leaves + 1) * rank, width), BF16),
            pltpu.SemaphoreType.DMA((2, groups)),
            pltpu.SemaphoreType.DMA((groups + 1,)),
            pltpu.SemaphoreType.DMA((6,)),
        ],
        name="moments",
        **settings(12, MOMENTS_WORK),
    )(*in_hbm(charges, basis, transfer3, transfer2, transfer1, coupling1, coupling0), after)


def upper_kernel(far1, far0, terms, below, own_coupling1, own_coupling0, spread):
    rank = below.shape[1]
    node = node_index()
    partners = far1.shape[1]
    source = far0[node // FAN] * FAN
    top = dot_t(
        jnp.concatenate([below[source + i] for i in range(FAN)], axis=0),
        jnp.concatenate([terms[source + i] for i in range(FAN)], axis=0),
    ).astype(BF16)
    local0 = dot(own_coupling0[0], top).astype(BF16)
    left = [own_coupling1[0, f] for f in range(partners)] + [below[node]]
    right = [terms[far1[node, f]] for f in range(partners)] + [local0]
    total = dot(jnp.concatenate(left, axis=1), jnp.concatenate(right, axis=0)).astype(BF16)
    for i in range(spread.shape[0]):
        spread[i] = total


def upper(far1, far0, terms, below, own_coupling1, own_coupling0):
    rank, width = terms.shape[1:]
    fellows = lax.axis_size("z")
    return pl.pallas_call(
        upper_kernel,
        in_specs=[SMEM, SMEM] + [VMEM] * 4,
        out_specs=VMEM,
        out_shape=jax.ShapeDtypeStruct((fellows, rank, width), BF16),
        name="upper",
        **settings(8, UPPER_WORK),
    )(far1, far0, terms, below, own_coupling1, own_coupling0)


def near_kernel(
    groups,
    near_list,
    first_edge,
    own,
    second_edge,
    mine,
    theirs,
    partial,
    charge_buf,
    mine_buf,
    theirs_buf,
    source_sems,
    sems,
):
    leaves, blocks, box, _ = mine.shape
    per = leaves // groups
    edge = first_edge.shape[0]
    device = device_index()
    odd = lax.rem(device, 2)
    first = device * leaves
    core = lax.axis_index("core")
    far_end = edge + leaves * box
    sources = [
        (first_edge, charge_buf.at[rows((1 - odd) * far_end, edge)]),
        (own, charge_buf.at[pl.ds(edge, leaves * box)]),
        (second_edge, charge_buf.at[rows(odd * far_end, edge)]),
    ]
    sources = [
        pltpu.make_async_copy(a, b, source_sems.at[i]) for i, (a, b) in enumerate(sources)
    ]

    def copies(i):
        part = pl.ds(i * per, per)
        return [
            pltpu.make_async_copy(mine.at[part], mine_buf.at[part], sems.at[0, i]),
            pltpu.make_async_copy(theirs.at[part], theirs_buf.at[part], sems.at[1, i]),
        ]

    def work(i):
        for j in range(per):
            leaf = i * per + j
            places = [near_list[leaf, core * blocks + s] for s in range(blocks)] + [
                near_list[leaf, (1 - core) * blocks + s] for s in range(blocks)
            ]
            left = jnp.concatenate(
                [mine_buf[leaf, s] for s in range(blocks)]
                + [theirs_buf[leaf, s] for s in range(blocks)],
                axis=1,
            )
            right = jnp.concatenate(
                [charge_buf[rows((place - first) * box + edge, box)] for place in places], axis=0
            )
            partial[rows(leaf * box, box)] = dot(left, right).astype(BF16)

    for copy in sources:
        copy.start()
    run = streamed(groups, 3, copies, work)
    for copy in sources:
        copy.wait()
    run()


def near_parts(near_list, first_edge, own, second_edge, mine, theirs):
    leaves, blocks, box, _ = mine.shape
    width = own.shape[1]
    groups = leaves // 4
    return pl.pallas_call(
        functools.partial(near_kernel, groups),
        in_specs=[SMEM] + [HBM] * 5,
        out_specs=VMEM,
        out_shape=jax.ShapeDtypeStruct((leaves * box, width), BF16),
        scratch_shapes=[
            pltpu.VMEM((2 * leaves * box, width), BF16),
            pltpu.VMEM(mine.shape, BF16),
            pltpu.VMEM(mine.shape, BF16),
            pltpu.SemaphoreType.DMA((3,)),
            pltpu.SemaphoreType.DMA((2, groups)),
        ],
        name="near_parts",
        **settings(24, NEAR_WORK),
    )(near_list, *in_hbm(first_edge, own, second_edge, mine, theirs))


def far_kernel(
    groups,
    far_list,
    after,
    first_message,
    message,
    second_message,
    coupling,
    result,
    moment_buf,
    coupling_buf,
    source_sems,
    sems,
):
    leaves, partners, rank, _ = coupling.shape
    per = leaves // groups
    tall = leaves * rank
    device = device_index()
    odd = lax.rem(device, 2)
    first = device * leaves
    sources = [
        (first_message.at[pl.ds(0, tall)], moment_buf.at[rows((1 - odd) * (2 * tall), tall)]),
        (message.at[pl.ds(0, tall)], moment_buf.at[pl.ds(tall, tall)]),
        (second_message.at[pl.ds(0, tall)], moment_buf.at[rows(odd * (2 * tall), tall)]),
    ]
    sources = [
        pltpu.make_async_copy(a, b, source_sems.at[i]) for i, (a, b) in enumerate(sources)
    ]

    def copies(i):
        part = pl.ds(i * per, per)
        return [pltpu.make_async_copy(coupling.at[part], coupling_buf.at[part], sems.at[i])]

    def work(i):
        for j in range(per):
            leaf = i * per + j
            left = jnp.concatenate([coupling_buf[leaf, f] for f in range(partners)], axis=1)
            right = jnp.concatenate(
                [
                    moment_buf[rows((far_list[leaf, f] - first + leaves) * rank, rank)]
                    for f in range(partners)
                ],
                axis=0,
            )
            result[rows(leaf * rank, rank)] = dot(left, right).astype(BF16)

    for copy in sources:
        copy.start()
    run = streamed(groups, 3, copies, work)
    for copy in sources:
        copy.wait()
    run()


def far_parts(far_list, after, first_message, message, second_message, coupling):
    leaves, partners, rank, _ = coupling.shape
    width = message.shape[1]
    groups = leaves // 4
    return pl.pallas_call(
        functools.partial(far_kernel, groups),
        in_specs=[SMEM] + [ANY] * 4 + [HBM],
        out_specs=VMEM,
        out_shape=jax.ShapeDtypeStruct((leaves * rank, width), BF16),
        scratch_shapes=[
            pltpu.VMEM((3 * leaves * rank, width), BF16),
            pltpu.VMEM(coupling.shape, BF16),
            pltpu.SemaphoreType.DMA((3,)),
            pltpu.SemaphoreType.DMA((groups,)),
        ],
        name="far_parts",
        **settings(16, FAR_WORK),
    )(far_list, after, first_message, message, second_message, *in_hbm(coupling))


def finish_kernel(
    groups,
    far2,
    pieces,
    near,
    far,
    first_message,
    second_message,
    first_two,
    second_two,
    coupling2,
    transfer2,
    transfer3,
    basis,
    potential,
    moment2_buf,
    coupling2_buf,
    transfer2_buf,
    transfer3_buf,
    basis_buf,
    result_buf,
    local_buf,
    sems,
    out_sems,
):
    leaves, box, rank = basis.shape
    per = leaves // groups
    fellows = pieces.shape[0]
    partners = far2.shape[1]
    first = [
        pltpu.make_async_copy(coupling2, coupling2_buf, sems.at[0]),
        pltpu.make_async_copy(transfer2, transfer2_buf, sems.at[1]),
    ]
    later = pltpu.make_async_copy(transfer3, transfer3_buf, sems.at[2])
    tall = leaves * rank
    device = device_index()
    odd = lax.rem(device, 2)
    upper_half = lax.rem(device, 4) // 2
    sides = [
        (first_message.at[pl.ds(tall, rank)], 3 - 2 * odd),
        (second_message.at[pl.ds(tall, rank)], 1 + 2 * odd),
        (first_two, 4 - 4 * upper_half),
        (second_two, 4 * upper_half),
    ]
    for i, (source, place) in enumerate(sides):
        target = moment2_buf.at[rows(place * rank, rank)]
        first.append(pltpu.make_async_copy(source, target, sems.at[3 + i]))

    def copies(i):
        part = pl.ds(i * per, per)
        return [pltpu.make_async_copy(basis.at[part], basis_buf.at[part], sems.at[7 + i])]

    def store(i):
        span = rows(i * (per * box), per * box)
        return pltpu.make_async_copy(result_buf.at[span], potential.at[span], out_sems.at[i])

    def work(i):
        for j in range(per):
            leaf = i * per + j
            span = rows(leaf * box, box)
            share = dot(basis_buf[leaf], local_buf[rows(leaf * rank, rank)])
            result_buf[span] = (near[span].astype(F32) + share).astype(BF16)
        store(i).start()

    for copy in first + [later]:
        copy.start()
    run = streamed(groups, groups, copies, work)
    total = pieces[0].astype(F32)
    for i in range(1, fellows):
        total = total + pieces[i].astype(F32)
    for copy in first:
        copy.wait()
    right = [moment2_buf[rows((far2[0, f] - device + 2) * rank, rank)] for f in range(partners)]
    right = jnp.concatenate(right + [total.astype(BF16)], axis=0)
    left = [coupling2_buf[0, f] for f in range(partners)] + [transfer2_buf[0]]
    local2 = dot(jnp.concatenate(left, axis=1), right).astype(BF16)
    later.wait()
    local_buf[...] = (far[...].astype(F32) + dot(transfer3_buf[...], local2)).astype(BF16)
    run()

    def finished(i, carry):
        store(i).wait()
        return carry

    lax.fori_loop(0, groups, finished, 0)


def finish(far2, pieces, near, far, sides, coupling2, transfer2, transfer3, basis):
    leaves, box, rank = basis.shape
    groups = 4
    return pl.pallas_call(
        functools.partial(finish_kernel, groups),
        in_specs=[SMEM] + [VMEM] * 3 + [ANY] * 4 + [HBM] * 4,
        out_specs=HBM,
        out_shape=jax.ShapeDtypeStruct(near.shape, BF16),
        scratch_shapes=[
            pltpu.VMEM((5 * rank, near.shape[1]), BF16),
            pltpu.VMEM(coupling2.shape, BF16),
            pltpu.VMEM(transfer2.shape, BF16),
            pltpu.VMEM(transfer3.shape, BF16),
            pltpu.VMEM(basis.shape, BF16),
            pltpu.VMEM(near.shape, BF16),
            pltpu.VMEM(far.shape, BF16),
            pltpu.SemaphoreType.DMA((7 + groups,)),
            pltpu.SemaphoreType.DMA((groups,)),
        ],
        name="finish",
        **settings(12),
    )(far2, pieces, near, far, *sides, *in_hbm(coupling2, transfer2, transfer3, basis))


def two_away(block, odd):
    count = lax.axis_size(LEAF)
    pairs = [(i, i + 2) for i in range(count - 2) if i // 2 % 2 == odd]
    return lax.ppermute(block, LEAF, pairs + [(b, a) for a, b in pairs])


def body(
    charges,
    leaf_basis,
    transfer3,
    transfer2,
    transfer1,
    coupling3,
    coupling2,
    coupling1,
    coupling0,
    near_blocks,
    near_list,
    far_list3,
    far_list2,
    far_list1,
    far_list0,
):
    leaves, box, width = charges.shape
    rank = leaf_basis.shape[2]
    other_blocks = swapped(near_blocks)
    flat = charges.reshape(leaves * box, width)
    transfer3 = transfer3.reshape(leaves * rank, rank)
    edge_one, edge_two = edges(flat)
    first_edge = exchanged(edge_one, False)
    second_edge = exchanged(edge_two, True)
    message, moment2, spread, *parts = moments(
        flat, leaf_basis, transfer3, transfer2, transfer1, coupling1, coupling0, edge_one
    )
    terms = lax.all_to_all(spread, ("y", "x"), 0, 0, tiled=True)
    first_message = exchanged(message, False)
    first_two = two_away(moment2, 0)
    second_two = two_away(moment2, 1)
    terms, first_edge, second_edge, first_two, second_two, late = lax.optimization_barrier(
        (terms, first_edge, second_edge, first_two, second_two, message)
    )
    second_message = exchanged(late, True)
    pieces = upper(far_list1, far_list0, terms, *parts)
    pieces = lax.all_to_all(pieces, "z", 0, 0, tiled=True)
    near = near_parts(near_list, first_edge, flat, second_edge, near_blocks, other_blocks)
    far = far_parts(far_list3, near, first_message, message, second_message, coupling3)
    sides = first_message, second_message, first_two, second_two
    potential = finish(far_list2, pieces, near, far, sides, coupling2, transfer2, transfer3, leaf_basis)
    return potential.reshape(leaves, box, width)


def solution(mesh):
    grid = Mesh(mesh.devices.reshape(4, 4, 8, 2), ("y", "x", "z", "core"))
    placed = (
        P(LEAF, None, "core"),
        P(LEAF, None, None),
        P(LEAF, None, None),
        P(LEAF, None, None),
        P(),
        P(LEAF, None, None, None),
        P(LEAF, None, None, None),
        P(),
        P(),
        P(LEAF, "core", None, None),
        P(LEAF, None),
        P(LEAF, None),
        P(LEAF, None),
        P(),
        P(),
    )
    return jax.shard_map(
        body, mesh=grid, in_specs=placed, out_specs=P(LEAF, None, "core"), check_vma=False
    )
```

```python
import functools

import jax
import jax.numpy as jnp
from jax import lax
from jax.experimental import pallas as pl
from jax.experimental.pallas import tpu as pltpu
from jax.sharding import Mesh, PartitionSpec as P

TOP1 = 16
TOP0 = 4
FAN = TOP1 // TOP0
LEAF = ("y", "x", "z")
F32 = jnp.float32
BF16 = jnp.bfloat16
MIB = 1024 * 1024
NEAR_WORK = 5
FAR_WORK = 20
UPPER_WORK = 5
MOMENTS_WORK = 1
HBM = pl.BlockSpec(memory_space=pltpu.HBM)
ANY = pl.BlockSpec(memory_space=pl.ANY)
VMEM = pl.BlockSpec(memory_space=pltpu.VMEM)
SMEM = pl.BlockSpec(memory_space=pltpu.SMEM)


def dot(a, b):
    return lax.dot_general(a, b, (((1,), (0,)), ((), ())), preferred_element_type=F32)


def dot_t(a, b):
    return lax.dot_general(a, b, (((0,), (0,)), ((), ())), preferred_element_type=F32)


def rows(start, size):
    return pl.ds(pl.multiple_of(start, 128), size)


def node_index():
    return lax.axis_index("y") * lax.axis_size("x") + lax.axis_index("x")


def device_index():
    return node_index() * lax.axis_size("z") + lax.axis_index("z")


def swapped(block):
    return lax.ppermute(block, "core", [(0, 1), (1, 0)])


def in_hbm(*arrays):
    return [pltpu.with_memory_space_constraint(array, pltpu.HBM) for array in arrays]


def exchanged(block, odd):
    count = lax.axis_size(LEAF)
    pairs = [(i, i + 1) for i in range(1 if odd else 0, count - 1, 2)]
    return lax.ppermute(block, LEAF, pairs + [(b, a) for a, b in pairs])


def settings(limit, work=1):
    return dict(
        compiler_params=pltpu.CompilerParams(vmem_limit_bytes=limit * MIB),
        cost_estimate=pl.CostEstimate(flops=work * 10**9, bytes_accessed=1000, transcendentals=0),
    )


def streamed(count, depth, copies, work):
    def begin(i):
        for copy in copies(i):
            copy.start()

    def step(i, carry):
        for copy in copies(i):
            copy.wait()
        pl.when(i + depth < count)(lambda: begin(i + depth))
        work(i)
        return carry

    def first(i, carry):
        begin(i)
        return carry

    lax.fori_loop(0, min(depth, count), first, 0)
    return lambda: lax.fori_loop(0, count, step, 0)


def edges_kernel(charges, first, second, sems):
    half = first.shape[0]
    odd = lax.rem(device_index(), 2)
    copies = [
        pltpu.make_async_copy(charges.at[rows((1 - odd) * half, half)], first, sems.at[0]),
        pltpu.make_async_copy(charges.at[rows(odd * half, half)], second, sems.at[1]),
    ]
    for copy in copies:
        copy.start()
    for copy in copies:
        copy.wait()


def edges(charges):
    half = charges.shape[0] // 2
    shape = jax.ShapeDtypeStruct((half, charges.shape[1]), BF16)
    return pl.pallas_call(
        edges_kernel,
        in_specs=[HBM],
        out_specs=[VMEM, VMEM],
        out_shape=[shape, shape],
        scratch_shapes=[pltpu.SemaphoreType.DMA((2,))],
        name="edges",
        **settings(8),
    )(*in_hbm(charges))


def moments_kernel(
    groups,
    charges,
    basis,
    transfer3,
    transfer2,
    transfer1,
    coupling1,
    coupling0,
    after,
    moment_out,
    moment2_out,
    spread,
    below,
    own_coupling1,
    own_coupling0,
    charge_buf,
    basis_buf,
    transfer3_buf,
    transfer2_buf,
    moment_buf,
    in_sems,
    out_sems,
    upper_sems,
):
    leaves, box, rank = basis.shape
    per = leaves // groups
    node = node_index()
    root = node // FAN
    loads = []
    for i in range(groups):
        span = pl.ds(i * per * box, per * box)
        part = pl.ds(i * per, per)
        loads.append(
            [
                pltpu.make_async_copy(charges.at[span], charge_buf.at[span], in_sems.at[0, i]),
                pltpu.make_async_copy(basis.at[part], basis_buf.at[part], in_sems.at[1, i]),
            ]
        )
    extra = [
        (transfer3, transfer3_buf),
        (transfer2, transfer2_buf),
        (transfer1, below),
        (coupling1.at[pl.ds(node, 1)], own_coupling1),
        (coupling0.at[pl.ds(root, 1)], own_coupling0),
    ]
    extra = [pltpu.make_async_copy(a, b, upper_sems.at[i]) for i, (a, b) in enumerate(extra)]
    for load in loads:
        for copy in load:
            copy.start()
    for copy in extra:
        copy.start()
    stores = []
    for i in range(groups):
        for copy in loads[i]:
            copy.wait()
        for leaf in range(i * per, (i + 1) * per):
            moment = dot_t(basis_buf[leaf], charge_buf[pl.ds(leaf * box, box)])
            moment_buf[pl.ds(leaf * rank, rank)] = moment.astype(BF16)
        span = pl.ds(i * per * rank, per * rank)
        copy = pltpu.make_async_copy(moment_buf.at[span], moment_out.at[span], out_sems.at[i])
        copy.start()
        stores.append(copy)
    for copy in extra[:2]:
        copy.wait()
    moment2 = dot_t(transfer3_buf[...], moment_buf[pl.ds(0, leaves * rank)]).astype(BF16)
    moment_buf[pl.ds(leaves * rank, rank)] = moment2
    span = pl.ds(leaves * rank, rank)
    copy = pltpu.make_async_copy(moment_buf.at[span], moment_out.at[span], out_sems.at[groups])
    copy.start()
    stores.append(copy)
    moment2_out[...] = moment2
    term = dot_t(transfer2_buf[0], moment2).astype(BF16)
    for i in range(spread.shape[0]):
        spread[i] = term
    for copy in stores + extra[2:]:
        copy.wait()


def moments(charges, basis, transfer3, transfer2, transfer1, coupling1, coupling0, after):
    leaves, box, rank = basis.shape
    width = charges.shape[1]
    partners = coupling1.shape[1]
    groups = 4
    return pl.pallas_call(
        functools.partial(moments_kernel, groups),
        in_specs=[HBM] * 7 + [ANY],
        out_specs=[ANY] + [VMEM] * 5,
        out_shape=[
            jax.ShapeDtypeStruct(((leaves + 1) * rank, width), BF16),
            jax.ShapeDtypeStruct((rank, width), BF16),
            jax.ShapeDtypeStruct((TOP1, rank, width), BF16),
            jax.ShapeDtypeStruct(transfer1.shape, BF16),
            jax.ShapeDtypeStruct((1, partners, rank, rank), BF16),
            jax.ShapeDtypeStruct((1, rank, rank), BF16),
        ],
        scratch_shapes=[
            pltpu.VMEM((leaves * box, width), BF16),
            pltpu.VMEM((leaves, box, rank), BF16),
            pltpu.VMEM((leaves * rank, rank), BF16),
            pltpu.VMEM((1, rank, rank), BF16),
            pltpu.VMEM(((leaves + 1) * rank, width), BF16),
            pltpu.SemaphoreType.DMA((2, groups)),
            pltpu.SemaphoreType.DMA((groups + 1,)),
            pltpu.SemaphoreType.DMA((6,)),
        ],
        name="moments",
        **settings(12, MOMENTS_WORK),
    )(*in_hbm(charges, basis, transfer3, transfer2, transfer1, coupling1, coupling0), after)


def upper_kernel(far1, far0, terms, below, own_coupling1, own_coupling0, spread):
    rank = below.shape[1]
    node = node_index()
    partners = far1.shape[1]
    source = far0[node // FAN] * FAN
    top = dot_t(
        jnp.concatenate([below[source + i] for i in range(FAN)], axis=0),
        jnp.concatenate([terms[source + i] for i in range(FAN)], axis=0),
    ).astype(BF16)
    local0 = dot(own_coupling0[0], top).astype(BF16)
    left = [own_coupling1[0, f] for f in range(partners)] + [below[node]]
    right = [terms[far1[node, f]] for f in range(partners)] + [local0]
    total = dot(jnp.concatenate(left, axis=1), jnp.concatenate(right, axis=0)).astype(BF16)
    for i in range(spread.shape[0]):
        spread[i] = total


def upper(far1, far0, terms, below, own_coupling1, own_coupling0):
    rank, width = terms.shape[1:]
    fellows = lax.axis_size("z")
    return pl.pallas_call(
        upper_kernel,
        in_specs=[SMEM, SMEM] + [VMEM] * 4,
        out_specs=VMEM,
        out_shape=jax.ShapeDtypeStruct((fellows, rank, width), BF16),
        name="upper",
        **settings(8, UPPER_WORK),
    )(far1, far0, terms, below, own_coupling1, own_coupling0)


def near_kernel(
    groups,
    near_list,
    first_edge,
    own,
    second_edge,
    mine,
    theirs,
    partial,
    charge_buf,
    mine_buf,
    theirs_buf,
    source_sems,
    sems,
):
    leaves, blocks, box, _ = mine.shape
    per = leaves // groups
    edge = first_edge.shape[0]
    device = device_index()
    odd = lax.rem(device, 2)
    first = device * leaves
    core = lax.axis_index("core")
    far_end = edge + leaves * box
    sources = [
        (first_edge, charge_buf.at[rows((1 - odd) * far_end, edge)]),
        (own, charge_buf.at[pl.ds(edge, leaves * box)]),
        (second_edge, charge_buf.at[rows(odd * far_end, edge)]),
    ]
    sources = [
        pltpu.make_async_copy(a, b, source_sems.at[i]) for i, (a, b) in enumerate(sources)
    ]

    def copies(i):
        part = pl.ds(i * per, per)
        return [
            pltpu.make_async_copy(mine.at[part], mine_buf.at[part], sems.at[0, i]),
            pltpu.make_async_copy(theirs.at[part], theirs_buf.at[part], sems.at[1, i]),
        ]

    def work(i):
        for j in range(per):
            leaf = i * per + j
            places = [near_list[leaf, core * blocks + s] for s in range(blocks)] + [
                near_list[leaf, (1 - core) * blocks + s] for s in range(blocks)
            ]
            left = jnp.concatenate(
                [mine_buf[leaf, s] for s in range(blocks)]
                + [theirs_buf[leaf, s] for s in range(blocks)],
                axis=1,
            )
            right = jnp.concatenate(
                [charge_buf[rows((place - first) * box + edge, box)] for place in places], axis=0
            )
            partial[rows(leaf * box, box)] = dot(left, right).astype(BF16)

    for copy in sources:
        copy.start()
    run = streamed(groups, 3, copies, work)
    for copy in sources:
        copy.wait()
    run()


def near_parts(near_list, first_edge, own, second_edge, mine, theirs):
    leaves, blocks, box, _ = mine.shape
    width = own.shape[1]
    groups = leaves // 4
    return pl.pallas_call(
        functools.partial(near_kernel, groups),
        in_specs=[SMEM] + [HBM] * 5,
        out_specs=VMEM,
        out_shape=jax.ShapeDtypeStruct((leaves * box, width), BF16),
        scratch_shapes=[
            pltpu.VMEM((2 * leaves * box, width), BF16),
            pltpu.VMEM(mine.shape, BF16),
            pltpu.VMEM(mine.shape, BF16),
            pltpu.SemaphoreType.DMA((3,)),
            pltpu.SemaphoreType.DMA((2, groups)),
        ],
        name="near_parts",
        **settings(24, NEAR_WORK),
    )(near_list, *in_hbm(first_edge, own, second_edge, mine, theirs))


def far_kernel(
    groups,
    far_list,
    after,
    first_message,
    message,
    second_message,
    coupling,
    result,
    moment_buf,
    coupling_buf,
    source_sems,
    sems,
):
    leaves, partners, rank, _ = coupling.shape
    per = leaves // groups
    tall = leaves * rank
    device = device_index()
    odd = lax.rem(device, 2)
    first = device * leaves
    sources = [
        (first_message.at[pl.ds(0, tall)], moment_buf.at[rows((1 - odd) * (2 * tall), tall)]),
        (message.at[pl.ds(0, tall)], moment_buf.at[pl.ds(tall, tall)]),
        (second_message.at[pl.ds(0, tall)], moment_buf.at[rows(odd * (2 * tall), tall)]),
    ]
    sources = [
        pltpu.make_async_copy(a, b, source_sems.at[i]) for i, (a, b) in enumerate(sources)
    ]

    def copies(i):
        part = pl.ds(i * per, per)
        return [pltpu.make_async_copy(coupling.at[part], coupling_buf.at[part], sems.at[i])]

    def work(i):
        for j in range(per):
            leaf = i * per + j
            left = jnp.concatenate([coupling_buf[leaf, f] for f in range(partners)], axis=1)
            right = jnp.concatenate(
                [
                    moment_buf[rows((far_list[leaf, f] - first + leaves) * rank, rank)]
                    for f in range(partners)
                ],
                axis=0,
            )
            result[rows(leaf * rank, rank)] = dot(left, right).astype(BF16)

    for copy in sources:
        copy.start()
    run = streamed(groups, 3, copies, work)
    for copy in sources:
        copy.wait()
    run()


def far_parts(far_list, after, first_message, message, second_message, coupling):
    leaves, partners, rank, _ = coupling.shape
    width = message.shape[1]
    groups = leaves // 4
    return pl.pallas_call(
        functools.partial(far_kernel, groups),
        in_specs=[SMEM] + [ANY] * 4 + [HBM],
        out_specs=VMEM,
        out_shape=jax.ShapeDtypeStruct((leaves * rank, width), BF16),
        scratch_shapes=[
            pltpu.VMEM((3 * leaves * rank, width), BF16),
            pltpu.VMEM(coupling.shape, BF16),
            pltpu.SemaphoreType.DMA((3,)),
            pltpu.SemaphoreType.DMA((groups,)),
        ],
        name="far_parts",
        **settings(16, FAR_WORK),
    )(far_list, after, first_message, message, second_message, *in_hbm(coupling))


def finish_kernel(
    groups,
    far2,
    pieces,
    near,
    far,
    first_message,
    second_message,
    first_two,
    second_two,
    coupling2,
    transfer2,
    transfer3,
    basis,
    potential,
    moment2_buf,
    coupling2_buf,
    transfer2_buf,
    transfer3_buf,
    basis_buf,
    result_buf,
    local_buf,
    sems,
    out_sems,
):
    leaves, box, rank = basis.shape
    per = leaves // groups
    fellows = pieces.shape[0]
    partners = far2.shape[1]
    first = [
        pltpu.make_async_copy(coupling2, coupling2_buf, sems.at[0]),
        pltpu.make_async_copy(transfer2, transfer2_buf, sems.at[1]),
    ]
    later = pltpu.make_async_copy(transfer3, transfer3_buf, sems.at[2])
    tall = leaves * rank
    device = device_index()
    odd = lax.rem(device, 2)
    upper_half = lax.rem(device, 4) // 2
    sides = [
        (first_message.at[pl.ds(tall, rank)], 3 - 2 * odd),
        (second_message.at[pl.ds(tall, rank)], 1 + 2 * odd),
        (first_two, 4 - 4 * upper_half),
        (second_two, 4 * upper_half),
    ]
    for i, (source, place) in enumerate(sides):
        target = moment2_buf.at[rows(place * rank, rank)]
        first.append(pltpu.make_async_copy(source, target, sems.at[3 + i]))

    def copies(i):
        part = pl.ds(i * per, per)
        return [pltpu.make_async_copy(basis.at[part], basis_buf.at[part], sems.at[7 + i])]

    def store(i):
        span = rows(i * (per * box), per * box)
        return pltpu.make_async_copy(result_buf.at[span], potential.at[span], out_sems.at[i])

    def work(i):
        for j in range(per):
            leaf = i * per + j
            span = rows(leaf * box, box)
            share = dot(basis_buf[leaf], local_buf[rows(leaf * rank, rank)])
            result_buf[span] = (near[span].astype(F32) + share).astype(BF16)
        store(i).start()

    for copy in first + [later]:
        copy.start()
    run = streamed(groups, groups, copies, work)
    total = pieces[0].astype(F32)
    for i in range(1, fellows):
        total = total + pieces[i].astype(F32)
    for copy in first:
        copy.wait()
    right = [moment2_buf[rows((far2[0, f] - device + 2) * rank, rank)] for f in range(partners)]
    right = jnp.concatenate(right + [total.astype(BF16)], axis=0)
    left = [coupling2_buf[0, f] for f in range(partners)] + [transfer2_buf[0]]
    local2 = dot(jnp.concatenate(left, axis=1), right).astype(BF16)
    later.wait()
    local_buf[...] = (far[...].astype(F32) + dot(transfer3_buf[...], local2)).astype(BF16)
    run()

    def finished(i, carry):
        store(i).wait()
        return carry

    lax.fori_loop(0, groups, finished, 0)


def finish(far2, pieces, near, far, sides, coupling2, transfer2, transfer3, basis):
    leaves, box, rank = basis.shape
    groups = 4
    return pl.pallas_call(
        functools.partial(finish_kernel, groups),
        in_specs=[SMEM] + [VMEM] * 3 + [ANY] * 4 + [HBM] * 4,
        out_specs=HBM,
        out_shape=jax.ShapeDtypeStruct(near.shape, BF16),
        scratch_shapes=[
            pltpu.VMEM((5 * rank, near.shape[1]), BF16),
            pltpu.VMEM(coupling2.shape, BF16),
            pltpu.VMEM(transfer2.shape, BF16),
            pltpu.VMEM(transfer3.shape, BF16),
            pltpu.VMEM(basis.shape, BF16),
            pltpu.VMEM(near.shape, BF16),
            pltpu.VMEM(far.shape, BF16),
            pltpu.SemaphoreType.DMA((7 + groups,)),
            pltpu.SemaphoreType.DMA((groups,)),
        ],
        name="finish",
        **settings(12),
    )(far2, pieces, near, far, *sides, *in_hbm(coupling2, transfer2, transfer3, basis))


def two_away(block, odd):
    count = lax.axis_size(LEAF)
    pairs = [(i, i + 2) for i in range(count - 2) if i // 2 % 2 == odd]
    return lax.ppermute(block, LEAF, pairs + [(b, a) for a, b in pairs])


def body(
    charges,
    leaf_basis,
    transfer3,
    transfer2,
    transfer1,
    coupling3,
    coupling2,
    coupling1,
    coupling0,
    near_blocks,
    near_list,
    far_list3,
    far_list2,
    far_list1,
    far_list0,
):
    leaves, box, width = charges.shape
    rank = leaf_basis.shape[2]
    other_blocks = swapped(near_blocks)
    flat = charges.reshape(leaves * box, width)
    transfer3 = transfer3.reshape(leaves * rank, rank)
    edge_one, edge_two = edges(flat)
    first_edge = exchanged(edge_one, False)
    second_edge = exchanged(edge_two, True)
    message, moment2, spread, *parts = moments(
        flat, leaf_basis, transfer3, transfer2, transfer1, coupling1, coupling0, edge_one
    )
    terms = lax.all_to_all(spread, ("y", "x"), 0, 0, tiled=True)
    first_message = exchanged(message, False)
    first_two = two_away(moment2, 0)
    second_two = two_away(moment2, 1)
    terms, first_edge, second_edge, late = lax.optimization_barrier(
        (terms, first_edge, second_edge, message)
    )
    second_message = exchanged(late, True)
    pieces = upper(far_list1, far_list0, terms, *parts)
    pieces = lax.all_to_all(pieces, "z", 0, 0, tiled=True)
    near = near_parts(near_list, first_edge, flat, second_edge, near_blocks, other_blocks)
    far = far_parts(far_list3, near, first_message, message, second_message, coupling3)
    sides = first_message, second_message, first_two, second_two
    potential = finish(far_list2, pieces, near, far, sides, coupling2, transfer2, transfer3, leaf_basis)
    return potential.reshape(leaves, box, width)


def solution(mesh):
    grid = Mesh(mesh.devices.reshape(4, 4, 8, 2), ("y", "x", "z", "core"))
    placed = (
        P(LEAF, None, "core"),
        P(LEAF, None, None),
        P(LEAF, None, None),
        P(LEAF, None, None),
        P(),
        P(LEAF, None, None, None),
        P(LEAF, None, None, None),
        P(),
        P(),
        P(LEAF, "core", None, None),
        P(LEAF, None),
        P(LEAF, None),
        P(LEAF, None),
        P(),
        P(),
    )
    return jax.shard_map(
        body, mesh=grid, in_specs=placed, out_specs=P(LEAF, None, "core"), check_vma=False
    )
```
